512 devices in a mesh: row: 16 (over y_lo, x, core), col: 32 (over z, y_hi).
Axes of the slice: x: 4, y: 4 (y_hi: 2, y_lo: 2; y = y_hi * 2 + y_lo), z: 16, core: 2. Of those that a mesh axis runs over, the one named last changes fastest.
Arguments:
- specimen: float32 [2, 4096, 8192], P(None, 'row', 'col'), may hold values from -5 to 5
- probe_modes: bfloat16 [4, 2, 256, 256], replicated, may hold values from -5 to 5
- amplitude: float32 [16, 32, 1, 256, 256], P('row', 'col'), may hold values from 0.5 to 4
- offsets: int32 [16, 32, 1, 2], P('row', 'col'), may hold values from 0 to 7936, as said below
- counts: int32 [16, 32], P('row', 'col'), may hold values from 0 to 1, as said below
Outputs:
- specimen_grad: float32 [2, 4096, 8192], P(None, 'row', 'col')
- probe_grad: float32 [4, 2, 256, 256], P(None, None, 'row', 'col')
The draws below stay inside these ranges and needn't reach their ends.
Inputs may be any that keep to these rules, and one draw needn't show every extreme that they name: offsets[a, b, s] = (r, c) satisfies a * 256 <= r < (a + 1) * 256, b * 256 <= c < (b + 1) * 256, r <= 3840 and c <= 7936: every patch lies inside the specimen and starts in its own tile. counts[a, b] is the number of live slots of tile (a, b); slots from counts[a, b] on carry drawn offsets and amplitudes that no output uses.
All inputs are finite; a program needn't handle non-finite values.
Results may differ from the reference program's by a relative error of at most 0.0079.
The reference program's roundings to bfloat16 on the way count: a program that leaves them out, or rounds other values in their place, can miss the bound.
Values sent between devices are 32-bit elements; how exact they have to be, the bound alone decides.
No kernel may reach another device: no remote copies, remote signals or barrier semaphores. Data moves between devices by JAX's collectives and lax.ppermute only.
A program may use at most 64 MiB of HBM per device.

```python
import math
import jax
import jax.numpy as jnp
from jax import lax

PATCH = 256
MODES = 4
TILE_R = 256
TILE_C = 256
SLOTS_DEV = 1
ROWS = 4096
COLS = 8192
SLOTS = 512
N_ROW = 16
N_COL = 32


def draw_offsets(key, part):
    key = jax.random.fold_in(key, 11)
    row_key, col_key = jax.random.split(key)
    band_count = ROWS // TILE_R
    tile_count = COLS // TILE_C
    band_index = jnp.arange(band_count, dtype=jnp.int32)[:, None, None]
    tile_index = jnp.arange(tile_count, dtype=jnp.int32)[None, :, None]
    slot_index = jnp.arange(SLOTS_DEV, dtype=jnp.int32)[None, None, :]
    row_span = jnp.minimum(TILE_R, ROWS - PATCH - band_index * TILE_R + 1)
    col_span = jnp.minimum(TILE_C, COLS - PATCH - tile_index * TILE_C + 1)
    grid_shape = (band_count, tile_count, SLOTS_DEV)
    rows_drawn = band_index * TILE_R + jax.random.randint(row_key, grid_shape, 0, jnp.broadcast_to(row_span, grid_shape))
    cols_drawn = tile_index * TILE_C + jax.random.randint(col_key, grid_shape, 0, jnp.broadcast_to(col_span, grid_shape))
    first_corner = (band_index == 0) & (tile_index == 0) & (slot_index == 0)
    last_corner = (band_index == band_count - 1) & (tile_index == tile_count - 1) & (slot_index == 0)
    rows_drawn = jnp.where(first_corner, 0, jnp.where(last_corner, ROWS - PATCH, rows_drawn))
    cols_drawn = jnp.where(first_corner, 0, jnp.where(last_corner, COLS - PATCH, cols_drawn))
    return jnp.stack([rows_drawn, cols_drawn], -1).astype(jnp.int32)


def draw_counts(key, part):
    key = jax.random.fold_in(key, 23)
    level_key, busy_key, quiet_key = jax.random.split(key, 3)
    band_count = ROWS // TILE_R
    tile_count = COLS // TILE_C
    band_index = jnp.arange(band_count, dtype=jnp.int32)[:, None]
    tile_index = jnp.arange(tile_count, dtype=jnp.int32)[None, :]
    ceiling = 1 + SLOTS_DEV * (band_index * tile_count + tile_index * band_count) // (2 * band_count * tile_count)
    grid_shape = (band_count, tile_count)
    drawn = jax.random.randint(level_key, grid_shape, 0, jnp.broadcast_to(ceiling + 1, grid_shape))
    flat_index = band_index * tile_count + tile_index
    tile_total = band_count * tile_count
    busiest = jax.random.randint(busy_key, (), 0, tile_total)
    quietest = (busiest + 1 + jax.random.randint(quiet_key, (), 0, tile_total - 1)) % tile_total
    drawn = jnp.where(flat_index == busiest, SLOTS_DEV, drawn)
    drawn = jnp.where(flat_index == quietest, 0, drawn)
    return drawn.astype(jnp.int32)


def block_scale(rng, shape, shards, low, high):
    def one(dim, blocks):
        draws = jax.random.uniform(jax.random.fold_in(jax.random.fold_in(rng, 6), dim), (blocks,), jnp.float32, low / len(shards), high / len(shards))
        return jnp.repeat(jnp.exp(draws), shape[dim] // blocks).reshape((-1,) + (1,) * (len(shape) - dim - 1))

    loudness = one(*shards[0])
    for cut in shards[1:]:
        loudness = loudness * one(*cut)
    return loudness


def normal_values(stream_key, shape, spread, most, pieces=(), kind=jnp.bfloat16):
    gain = block_scale(stream_key, shape, pieces, -0.22, 0.18) if pieces else 1.0
    values = jax.random.normal(stream_key, shape, jnp.float32) * spread * gain
    return jnp.minimum(jnp.maximum(values, -most), most).astype(kind)


def setup_inputs(seed: int = 0) -> dict:
    arg_keys = jax.random.split(jax.random.key(seed), 6)
    return {
        "specimen": normal_values(arg_keys[0], (2, ROWS, COLS), 0.7, 5.0, ((1, 16), (2, 32)), jnp.float32),
        "probe_modes": normal_values(arg_keys[1], (MODES, 2, PATCH, PATCH), 0.7, 5.0),
        "amplitude": jnp.clip(jnp.exp(math.log(4.0) - 2.0794415 * jax.random.uniform(arg_keys[2], (N_ROW, N_COL, SLOTS_DEV, PATCH, PATCH), jnp.float32) ** block_scale(arg_keys[2], (N_ROW, N_COL, SLOTS_DEV, PATCH, PATCH), ((0, 16), (1, 32)), -0.2, 0.2)), 0.5, 4.0),
        "offsets": draw_offsets(jax.random.fold_in(arg_keys[5], 71), 0),
        "counts": draw_counts(jax.random.fold_in(arg_keys[5], 71), 0),
    }


def dft_tables(length, imag_sign):
    sample_index = jnp.arange(length, dtype=jnp.int32)
    phase_angle = (sample_index[:, None] * sample_index[None, :] % length).astype(jnp.float32) * (2.0 * math.pi / length)
    factor = 1.0 / math.sqrt(length)
    real_part = (jnp.cos(phase_angle) * factor).astype(jnp.bfloat16)
    imag_part = (imag_sign * jnp.sin(phase_angle) * factor).astype(jnp.bfloat16)
    left_table = jnp.concatenate([jnp.concatenate([real_part, -imag_part], 1), jnp.concatenate([imag_part, real_part], 1)], 0)
    right_table = jnp.stack([jnp.stack([real_part, imag_part], 1), jnp.stack([-imag_part, real_part], 1)], 0)
    return (left_table, right_table)

def transform(fields, left_table, right_table):
    mode_count = fields.shape[0]
    length = fields.shape[2]
    stacked = fields.astype(jnp.float32).reshape(mode_count, 2 * length, length)
    midway = jnp.einsum('xb,mbq->mxq', left_table.astype(jnp.float32), stacked).astype(jnp.bfloat16)
    midway = midway.astype(jnp.float32).reshape(mode_count, 2, length, length)
    return jnp.einsum('mrpq,rqst->mspt', midway, right_table.astype(jnp.float32))

def slot_terms(patch_field, illumination, amplitude_slot, forward, inverse):
    real_exit = illumination[:, 0] * patch_field[0] - illumination[:, 1] * patch_field[1]
    imag_exit = illumination[:, 0] * patch_field[1] + illumination[:, 1] * patch_field[0]
    exit_wave = jnp.stack([real_exit, imag_exit], 1)
    far_field = transform(exit_wave.astype(jnp.bfloat16), forward[0], forward[1])
    modulus = jnp.sqrt(lax.optimization_barrier(jnp.sum(far_field * far_field, axis=(0, 1))))
    rescale = amplitude_slot / jnp.maximum(modulus, 0.5)
    projected = transform((far_field * rescale).astype(jnp.bfloat16), inverse[0], inverse[1])
    residual_wave = exit_wave - projected
    spec_real = lax.optimization_barrier(jnp.sum(illumination[:, 0] * residual_wave[:, 0] + illumination[:, 1] * residual_wave[:, 1], 0))
    spec_imag = lax.optimization_barrier(jnp.sum(illumination[:, 0] * residual_wave[:, 1] - illumination[:, 1] * residual_wave[:, 0], 0))
    probe_real = patch_field[0] * residual_wave[:, 0] + patch_field[1] * residual_wave[:, 1]
    probe_imag = patch_field[0] * residual_wave[:, 1] - patch_field[1] * residual_wave[:, 0]
    return (jnp.stack([spec_real, spec_imag]), jnp.stack([probe_real, probe_imag], 1))

def reference(specimen, probe_modes, amplitude, offsets, counts):
    forward = dft_tables(PATCH, -1.0)
    inverse = dft_tables(PATCH, 1.0)
    illumination = probe_modes.astype(jnp.float32)
    flat_offsets = offsets.reshape(-1, 2).astype(jnp.int32)
    flat_amplitude = amplitude.reshape(-1, PATCH, PATCH)
    slot_numbers = jnp.arange(SLOTS_DEV, dtype=jnp.int32)
    live_weight = (slot_numbers[None, None, :] < counts[:, :, None]).astype(jnp.float32).reshape(-1)

    def one_slot(running, inputs):
        spec_acc, probe_acc = running
        corner, amplitude_slot, weight = inputs
        start_row = corner[0].astype(jnp.int32)
        start_col = corner[1].astype(jnp.int32)
        zero_index = jnp.zeros((), jnp.int32)
        patch_field = lax.dynamic_slice(specimen, (zero_index, start_row, start_col), (2, PATCH, PATCH))
        spec_term, probe_term = slot_terms(patch_field, illumination, amplitude_slot, forward, inverse)
        window_old = lax.dynamic_slice(spec_acc, (zero_index, start_row, start_col), (2, PATCH, PATCH))
        spec_acc = lax.dynamic_update_slice(spec_acc, window_old + weight * spec_term, (zero_index, start_row, start_col))
        return ((spec_acc, probe_acc + weight * probe_term), None)
    start_state = (jnp.zeros((2, ROWS, COLS), jnp.float32), jnp.zeros((MODES, 2, PATCH, PATCH), jnp.float32))
    (spec_acc, probe_acc), _ = lax.scan(one_slot, start_state, (flat_offsets, flat_amplitude, live_weight))
    return (spec_acc, probe_acc / SLOTS)
```

```python
import functools
import math

import jax
import jax.numpy as jnp
import ml_dtypes
import numpy as np
from jax import lax
from jax.experimental import pallas as pl
from jax.experimental.pallas import tpu as pltpu
from jax.sharding import PartitionSpec as P


def shifted(value, axis, steps):
    count = lax.axis_size(axis)
    first, last = (max(0, -steps), min(count, count - steps))
    return lax.ppermute(value, axis, [(source, source + steps) for source in range(first, last)])


def dft_tables(length):
    index = np.arange(length, dtype=np.int32)
    phase = (index[:, None] * index[None, :] % length).astype(np.float32) * np.float32(2.0 * math.pi / length)
    factor = np.float32(1.0 / math.sqrt(length))
    real = (np.cos(phase) * factor).astype(ml_dtypes.bfloat16)
    imag = (-np.sin(phase) * factor).astype(ml_dtypes.bfloat16)
    table_a = np.block([[real, imag], [-imag, real]])
    table_b = np.block([[real, -imag], [imag, real]])
    return table_a, table_b


def patch_kernel(
    scal_ref, own_ref, below_ref, beside_ref, probe_ref, amp_ref, ta_ref, tb_ref,
    keep_ref, send_ref, grad_ref,
    patch_s, far_s, grad_s,
):
    modes = probe_ref.shape[0]
    n = own_ref.shape[1]
    row0, col0, live, parity = scal_ref[0], scal_ref[1], scal_ref[2], scal_ref[3]
    rows = lax.broadcasted_iota(jnp.int32, (n, n), 0)
    cols = lax.broadcasted_iota(jnp.int32, (n, n), 1)
    for k in range(2):
        mixed = jnp.where(cols >= col0, jnp.where(rows >= row0, own_ref[k], below_ref[k]), beside_ref[k])
        mixed = pltpu.roll(mixed, (n - row0) % n, 0)
        patch_s[k] = pltpu.roll(mixed, (n - col0) % n, 1)
    power = jnp.zeros((n, n), jnp.float32)
    for m in range(modes):
        pr = probe_ref[m, 0].astype(jnp.float32)
        pi = probe_ref[m, 1].astype(jnp.float32)
        xr, xi = patch_s[0], patch_s[1]
        er = (pr * xr - pi * xi).astype(jnp.bfloat16)
        ei = (pr * xi + pi * xr).astype(jnp.bfloat16)
        low = jnp.concatenate([er, ei], 0)
        mid = jnp.dot(tb_ref[...], low, preferred_element_type=jnp.float32).astype(jnp.bfloat16)
        mid = jnp.concatenate([mid[:n], mid[n:]], 1)
        far = jnp.dot(mid, ta_ref[...], preferred_element_type=jnp.float32)
        far_s[m] = far
        power = power + (far[:, :n] * far[:, :n] + far[:, n:] * far[:, n:])
    scale = amp_ref[...] / jnp.maximum(jnp.sqrt(power), 0.5)
    for m in range(modes):
        fr = (far_s[m, :, :n] * scale).astype(jnp.bfloat16)
        fi = (far_s[m, :, n:] * scale).astype(jnp.bfloat16)
        low = jnp.concatenate([fr, fi], 0)
        mid = jnp.dot(ta_ref[...], low, preferred_element_type=jnp.float32).astype(jnp.bfloat16)
        mid = jnp.concatenate([mid[:n], mid[n:]], 1)
        far_s[m] = jnp.dot(mid, tb_ref[...], preferred_element_type=jnp.float32)
    live_f = live.astype(jnp.float32)
    part = keep_ref.shape[1] // (2 * modes)
    mean = live_f * scal_ref[4].astype(jnp.float32)
    inverse = 1.0 / scal_ref[5].astype(jnp.float32)
    for a in range(keep_ref.shape[0]):
        for q, out_ref in ((0, keep_ref), (1, send_ref)):
            half = parity if q == 0 else 1 - parity
            here = pl.ds(pl.multiple_of(a * 2 * part + half * part, part), part)
            xr, xi = patch_s[0, here, :], patch_s[1, here, :]
            sr, si = xr * (mean * inverse), xi * (mean * inverse)
            gr = jnp.zeros_like(xr)
            gi = jnp.zeros_like(xr)
            for m in range(modes):
                pr = probe_ref[m, 0, here, :].astype(jnp.float32)
                pi = probe_ref[m, 1, here, :].astype(jnp.float32)
                dr = (pr * xr - pi * xi) - far_s[m, here, :n]
                di = (pr * xi + pi * xr) - far_s[m, here, n:]
                gr = gr + (pr * dr + pi * di)
                gi = gi + (pr * di - pi * dr)
                out_ref[a, 2 * m * part:(2 * m + 1) * part, :] = sr * dr + si * di
                out_ref[a, (2 * m + 1) * part:(2 * m + 2) * part, :] = sr * di - si * dr
            grad_s[0, here, :] = gr * live_f
            grad_s[1, here, :] = gi * live_f
    for k in range(2):
        grad_ref[k] = pltpu.roll(pltpu.roll(grad_s[k], row0, 0), col0, 1)


def shards(specimen, probe_modes, amplitude, offsets, counts):
    tile_rows, tile_cols = specimen.shape[1:]
    modes = probe_modes.shape[0]
    n = probe_modes.shape[2]
    n_row, n_col = lax.axis_size("row"), lax.axis_size("col")
    slots = n_row * n_col * offsets.shape[2]
    row_id, col_id = lax.axis_index("row"), lax.axis_index("col")
    half = n_row // 2
    part = n // n_row

    corner = offsets[0, 0, 0] - jnp.stack([row_id * tile_rows, col_id * tile_cols])
    live = (counts[0, 0] > 0).astype(jnp.int32)
    row0, col0 = corner[0], corner[1]
    left_corner = shifted(corner, "col", 1)
    left_row, left_col = left_corner[0], left_corner[1]

    rows = lax.broadcasted_iota(jnp.int32, (1, n, n), 1)
    cols = lax.broadcasted_iota(jnp.int32, (1, n, n), 2)
    below = shifted(specimen, "row", -1)
    beside = shifted(jnp.where(rows >= left_row, specimen, below), "col", -1)

    table_a, table_b = dft_tables(n)
    parity = row_id % 2
    scalars = jnp.stack([row0, col0, live, parity, jnp.int32(1), jnp.int32(slots)]).astype(jnp.int32)
    vmem = pl.BlockSpec(memory_space=pltpu.VMEM)
    keep, send, grad = pl.pallas_call(
        patch_kernel,
        out_shape=(
            jax.ShapeDtypeStruct((half, 2 * modes * part, n), jnp.float32),
            jax.ShapeDtypeStruct((half, 2 * modes * part, n), jnp.float32),
            jax.ShapeDtypeStruct((2, n, n), jnp.float32),
        ),
        in_specs=[pl.BlockSpec(memory_space=pltpu.SMEM)] + [vmem] * 7,
        out_specs=(vmem, vmem, vmem),
        scratch_shapes=[
            pltpu.VMEM((2, n, n), jnp.float32),
            pltpu.VMEM((modes, n, 2 * n), jnp.float32),
            pltpu.VMEM((2, n, n), jnp.float32),
        ],
        compiler_params=pltpu.CompilerParams(vmem_limit_bytes=40 * 1024 * 1024),
    )(scalars, specimen, below, beside, probe_modes, amplitude[0, 0, 0], jnp.asarray(table_a), jnp.asarray(table_b))

    from_left = shifted(grad, "col", 1)
    mine = jnp.where(cols >= col0, grad, 0.0)
    theirs = jnp.where(cols < left_col, from_left, 0.0)
    down = jnp.where(rows < row0, mine, 0.0) + jnp.where(rows < left_row, theirs, 0.0)
    from_above = shifted(down, "row", 1)
    specimen_grad = (
        jnp.where(rows >= row0, mine, 0.0) + jnp.where(rows >= left_row, theirs, 0.0) + from_above
    )

    other = lax.ppermute(send, "row", [(i, i ^ 1) for i in range(n_row)])
    groups = [[i for i in range(n_row) if i % 2 == k] for k in range(2)]
    summed = lax.all_to_all(keep + other, "row", 0, 0, axis_index_groups=groups, tiled=True).sum(0)
    summed = summed.T.reshape(n_col, n // n_col, 2 * modes * part)
    summed = lax.all_to_all(summed, "col", 0, 0, tiled=True).sum(0)
    probe_grad = summed.T.reshape(modes, 2, part, n // n_col)
    return (specimen_grad, probe_grad)


def solution(mesh):
    in_specs = (
        P(None, "row", "col"),
        P(),
        P("row", "col", None, None, None),
        P("row", "col", None, None),
        P("row", "col"),
    )
    out_specs = (P(None, "row", "col"), P(None, None, "row", "col"))
    return jax.shard_map(shards, mesh=mesh, in_specs=in_specs, out_specs=out_specs, check_vma=False)
```

```python
import functools
import math

import jax
import jax.numpy as jnp
import ml_dtypes
import numpy as np
from jax import lax
from jax.experimental import pallas as pl
from jax.experimental.pallas import tpu as pltpu
from jax.sharding import Mesh
from jax.sharding import PartitionSpec as P

ROW = ("ylo", "x", "core")
COL = ("z", "yhi")
FIRST_ROWS = 144


def shifted(value, axis, steps):
    count = lax.axis_size(axis)
    first, last = (max(0, -steps), min(count, count - steps))
    return lax.ppermute(value, axis, [(source, source + steps) for source in range(first, last)])


def dft_tables(length):
    index = np.arange(length, dtype=np.int32)
    phase = (index[:, None] * index[None, :] % length).astype(np.float32) * np.float32(2.0 * math.pi / length)
    factor = np.float32(1.0 / math.sqrt(length))
    real = (np.cos(phase) * factor).astype(ml_dtypes.bfloat16)
    imag = (-np.sin(phase) * factor).astype(ml_dtypes.bfloat16)
    return np.block([[real, imag], [-imag, real]]), np.block([[real, -imag], [imag, real]])


def mix_kernel(corner_ref, own_ref, right_ref, out_ref):
    cols = lax.broadcasted_iota(jnp.int32, own_ref.shape, 2)
    out_ref[...] = jnp.where(cols >= corner_ref[1], own_ref[...], right_ref[...])


def side_kernel(scal_ref, own0_ref, own1_ref, right0_ref, right1_ref, probe_in, amp_in, ta_in, tb_in,
                side_ref, probe_ref, amp_ref, ta_ref, tb_ref):
    first = own0_ref.shape[1]
    cols = lax.broadcasted_iota(jnp.int32, side_ref.shape, 2)
    side_ref[:, :first] = jnp.where(cols[:, :first] >= scal_ref[1], own0_ref[...], right0_ref[...])
    side_ref[:, first:] = jnp.where(cols[:, first:] >= scal_ref[1], own1_ref[...], right1_ref[...])
    for src, dst in ((probe_in, probe_ref), (amp_in, amp_ref), (ta_in, ta_ref), (tb_in, tb_ref)):
        dst[...] = src[...]


def split_kernel(scal_ref, grad_ref, left_ref, mine_ref, down_ref):
    n = mine_ref.shape[1]
    row0, col0 = scal_ref[0], scal_ref[1]
    rows = lax.broadcasted_iota(jnp.int32, (n, n), 0)
    cols = lax.broadcasted_iota(jnp.int32, (n, n), 1)
    left_rows = rows.astype(jnp.float32) >= left_ref[0, n:n + 1]
    left_cols = cols.astype(jnp.float32) < left_ref[1, n:n + 1]
    for k in range(2):
        own = jnp.where(cols >= col0, grad_ref[k, :n], 0.0)
        left = jnp.where(left_cols, left_ref[k, :n], 0.0)
        mine_ref[k] = jnp.where(rows >= row0, own, 0.0) + jnp.where(left_rows, left, 0.0)
        down_ref[k] = jnp.where(rows < row0, own, 0.0) + jnp.where(left_rows, 0.0, left)


def pair_kernel(keep_ref, other_ref, out_ref):
    count, wide, n = keep_ref.shape
    n_x, _, n_y, n_z, eight = out_ref.shape[:5]
    for a in range(count):
        turned = (keep_ref[a] + other_ref[a]).T.reshape(n_z, 2, eight, wide)
        out_ref[a % n_x, 0, a // n_x] = turned[:, 0]
        out_ref[a % n_x, 1, a // n_x] = turned[:, 1]


def patch_kernel(
    inverse_slots, scal_ref, side_ref, under0_ref, under1_ref, probe_ref, amp_ref, ta_ref, tb_ref,
    keep_ref, send_ref, grad_ref,
    patch_s, far_s, grad_s, mid_s,
):
    modes = probe_ref.shape[0]
    n = side_ref.shape[1]
    row0, col0, live, parity = scal_ref[0], scal_ref[1], scal_ref[2], scal_ref[3]
    rows = lax.broadcasted_iota(jnp.int32, (n, n), 0)
    for k in range(2):
        under = jnp.concatenate([under0_ref[k], under1_ref[k]], 0)
        mixed = jnp.where(rows >= row0, side_ref[k], under)
        mixed = pltpu.roll(mixed, (n - row0) % n, 0)
        patch_s[k] = pltpu.roll(mixed, (n - col0) % n, 1)
    xr, xi = patch_s[0], patch_s[1]
    for m in range(modes):
        pr = probe_ref[m, 0].astype(jnp.float32)
        pi = probe_ref[m, 1].astype(jnp.float32)
        er = (pr * xr - pi * xi).astype(jnp.bfloat16)
        ei = (pr * xi + pi * xr).astype(jnp.bfloat16)
        mid = jnp.dot(tb_ref[...], jnp.concatenate([er, ei], 0), preferred_element_type=jnp.float32)
        mid_s[m * n:(m + 1) * n, :n] = mid[:n].astype(jnp.bfloat16)
        mid_s[m * n:(m + 1) * n, n:] = mid[n:].astype(jnp.bfloat16)
    far_s[...] = jnp.dot(mid_s[...], ta_ref[...], preferred_element_type=jnp.float32).reshape(modes, n, 2 * n)
    power = jnp.zeros((n, n), jnp.float32)
    for m in range(modes):
        power = power + (far_s[m, :, :n] * far_s[m, :, :n] + far_s[m, :, n:] * far_s[m, :, n:])
    scale = amp_ref[...] / jnp.maximum(jnp.sqrt(power), 0.5)
    for m in range(modes):
        fr = (far_s[m, :, :n] * scale).astype(jnp.bfloat16)
        fi = (far_s[m, :, n:] * scale).astype(jnp.bfloat16)
        mid = jnp.dot(ta_ref[...], jnp.concatenate([fr, fi], 0), preferred_element_type=jnp.float32)
        mid_s[m * n:(m + 1) * n, :n] = mid[:n].astype(jnp.bfloat16)
        mid_s[m * n:(m + 1) * n, n:] = mid[n:].astype(jnp.bfloat16)
    far_s[...] = jnp.dot(mid_s[...], tb_ref[...], preferred_element_type=jnp.float32).reshape(modes, n, 2 * n)
    live_f = live.astype(jnp.float32)
    part = keep_ref.shape[1] // (2 * modes)
    mean = live_f * inverse_slots
    for a in range(keep_ref.shape[0]):
        for q, out_ref in ((0, keep_ref), (1, send_ref)):
            half = parity if q == 0 else 1 - parity
            here = pl.ds(pl.multiple_of(a * 2 * part + half * part, part), part)
            xr, xi = patch_s[0, here, :], patch_s[1, here, :]
            sr, si = xr * mean, xi * mean
            gr = jnp.zeros_like(xr)
            gi = jnp.zeros_like(xr)
            for m in range(modes):
                pr = probe_ref[m, 0, here, :].astype(jnp.float32)
                pi = probe_ref[m, 1, here, :].astype(jnp.float32)
                dr = (pr * xr - pi * xi) - far_s[m, here, :n]
                di = (pr * xi + pi * xr) - far_s[m, here, n:]
                gr = gr + (pr * dr + pi * di)
                gi = gi + (pr * di - pi * dr)
                out_ref[a, 2 * m * part:(2 * m + 1) * part, :] = sr * dr + si * di
                out_ref[a, (2 * m + 1) * part:(2 * m + 2) * part, :] = sr * di - si * dr
            grad_s[0, here, :] = gr * live_f
            grad_s[1, here, :] = gi * live_f
    for k in range(2):
        grad_ref[k, :n] = pltpu.roll(pltpu.roll(grad_s[k], row0, 0), col0, 1)
        grad_ref[k, n:] = jnp.full((grad_ref.shape[1] - n, n), scal_ref[k], jnp.int32).astype(jnp.float32)


def shards(specimen, probe_modes, amplitude, offsets, counts):
    tile_rows, tile_cols = specimen.shape[1:]
    modes = probe_modes.shape[0]
    n = probe_modes.shape[2]
    n_row, n_col = lax.axis_size(ROW), lax.axis_size(COL)
    slots = n_row * n_col * offsets.shape[2]
    row_id, col_id = lax.axis_index(ROW), lax.axis_index(COL)
    n_x, half = lax.axis_size("x"), n_row // 2
    part = n // n_row

    corner = offsets[0, 0, 0] - jnp.stack([row_id * tile_rows, col_id * tile_cols])
    live = (counts[0, 0] > 0).astype(jnp.int32)
    row0, col0 = corner[0], corner[1]

    own = [specimen[:, :FIRST_ROWS], lax.optimization_barrier(specimen)[:, FIRST_ROWS:]]
    right = [shifted(part_rows, COL, -1) for part_rows in own]
    vmem = pl.BlockSpec(memory_space=pltpu.VMEM)
    smem = pl.BlockSpec(memory_space=pltpu.SMEM)
    above_corner = shifted(corner, ROW, 1)
    mixed = [
        pl.pallas_call(
            mix_kernel,
            out_shape=jax.ShapeDtypeStruct(mine.shape, jnp.float32),
            in_specs=[smem, vmem, vmem],
            out_specs=vmem,
            compiler_params=pltpu.CompilerParams(vmem_limit_bytes=2 << 20),
        )(above_corner, mine, beside)
        for mine, beside in zip(own, right)
    ]
    under = [shifted(part_rows, ROW, -1) for part_rows in mixed]

    scalars = jnp.stack([row0, col0, live, row_id % 2]).astype(jnp.int32)
    table_a, table_b = dft_tables(n)
    operands = (probe_modes, amplitude[0, 0, 0], jnp.asarray(table_a), jnp.asarray(table_b))
    side, *operands = pl.pallas_call(
        side_kernel,
        out_shape=(jax.ShapeDtypeStruct((2, n, n), jnp.float32),)
        + tuple(jax.ShapeDtypeStruct(value.shape, value.dtype) for value in operands),
        in_specs=[smem] + [vmem] * 8,
        out_specs=(vmem,) * 5,
        compiler_params=pltpu.CompilerParams(vmem_limit_bytes=10 << 20),
    )(scalars, *own, *right, *operands)
    keep, send, grad = pl.pallas_call(
        functools.partial(patch_kernel, 1.0 / slots),
        out_shape=(
            jax.ShapeDtypeStruct((half, 2 * modes * part, n), jnp.float32),
            jax.ShapeDtypeStruct((half, 2 * modes * part, n), jnp.float32),
            jax.ShapeDtypeStruct((2, n + 8, n), jnp.float32),
        ),
        in_specs=[smem] + [vmem] * 7,
        out_specs=(vmem,) * 3,
        scratch_shapes=[
            pltpu.VMEM((2, n, n), jnp.float32),
            pltpu.VMEM((modes, n, 2 * n), jnp.float32),
            pltpu.VMEM((2, n, n), jnp.float32),
            pltpu.VMEM((modes * n, 2 * n), jnp.bfloat16),
        ],
        compiler_params=pltpu.CompilerParams(vmem_limit_bytes=14 << 20),
    )(scalars, side, *under, *operands)

    other = lax.ppermute(send, "core", [(0, 1), (1, 0)])
    from_left = shifted(grad, COL, 1)
    summed = pl.pallas_call(
        pair_kernel,
        out_shape=jax.ShapeDtypeStruct((n_x, 2, half // n_x, n_col // 2, n // n_col, 2 * modes * part), jnp.float32),
        in_specs=[vmem] * 2,
        out_specs=vmem,
        compiler_params=pltpu.CompilerParams(vmem_limit_bytes=8 << 20),
    )(keep, other)
    summed = lax.all_to_all(summed, "x", 0, 0, tiled=True)
    mine, down = pl.pallas_call(
        split_kernel,
        out_shape=(jax.ShapeDtypeStruct((2, n, n), jnp.float32),) * 2,
        in_specs=[smem, vmem, vmem],
        out_specs=(vmem,) * 2,
        compiler_params=pltpu.CompilerParams(vmem_limit_bytes=4 << 20),
    )(scalars, grad, from_left)
    from_above = shifted(down, ROW, 1)
    summed = summed.sum(0).reshape((2 * n_col,) + summed.shape[-2:])
    summed = lax.all_to_all(summed, ("yhi", "ylo", "z"), 0, 0, tiled=True).sum(0)
    probe_grad = summed.T.reshape(modes, 2, part, n // n_col)
    specimen_grad = mine + from_above
    return (specimen_grad, probe_grad)


def solution(mesh):
    n_row, n_col = mesh.devices.shape
    fine = Mesh(mesh.devices.reshape(2, n_row // 4, 2, n_col // 2, 2), ROW + COL)
    in_specs = (
        P(None, ROW, COL),
        P(),
        P(ROW, COL, None, None, None),
        P(ROW, COL, None, None),
        P(ROW, COL),
    )
    out_specs = (P(None, ROW, COL), P(None, None, ROW, COL))
    return jax.shard_map(shards, mesh=fine, in_specs=in_specs, out_specs=out_specs, check_vma=False)
```

```python
import functools
import math

import jax
import jax.numpy as jnp
import ml_dtypes
import numpy as np
from jax import lax
from jax.experimental import pallas as pl
from jax.experimental.pallas import tpu as pltpu
from jax.sharding import Mesh
from jax.sharding import PartitionSpec as P

ROW = ("ylo", "x", "core")
COL = ("z", "yhi")


def shifted(value, axis, steps):
    count = lax.axis_size(axis)
    first, last = (max(0, -steps), min(count, count - steps))
    return lax.ppermute(value, axis, [(source, source + steps) for source in range(first, last)])


def dft_tables(length):
    index = np.arange(length, dtype=np.int32)
    phase = (index[:, None] * index[None, :] % length).astype(np.float32) * np.float32(2.0 * math.pi / length)
    factor = np.float32(1.0 / math.sqrt(length))
    real = (np.cos(phase) * factor).astype(ml_dtypes.bfloat16)
    imag = (-np.sin(phase) * factor).astype(ml_dtypes.bfloat16)
    return np.block([[real, imag], [-imag, real]]), np.block([[real, -imag], [imag, real]])


def near_kernel(value_ref, out_ref):
    out_ref[...] = value_ref[...]


def mix_kernel(corner_ref, own_ref, below_ref, out_ref):
    rows = lax.broadcasted_iota(jnp.int32, own_ref.shape, 1)
    out_ref[...] = jnp.where(rows >= corner_ref[0], own_ref[...], below_ref[...])


def side_kernel(scal_ref, own_ref, below_ref, probe_in, amp_in, ta_in, tb_in,
                side_ref, probe_ref, amp_ref, ta_ref, tb_ref):
    rows = lax.broadcasted_iota(jnp.int32, own_ref.shape, 1)
    side_ref[...] = jnp.where(rows >= scal_ref[0], own_ref[...], below_ref[...])
    for src, dst in ((probe_in, probe_ref), (amp_in, amp_ref), (ta_in, ta_ref), (tb_in, tb_ref)):
        dst[...] = src[...]


def split_kernel(scal_ref, grad_ref, left_ref, mine_ref, down_ref):
    n = mine_ref.shape[1]
    row0, col0 = scal_ref[0], scal_ref[1]
    rows = lax.broadcasted_iota(jnp.int32, (n, n), 0)
    cols = lax.broadcasted_iota(jnp.int32, (n, n), 1)
    left_rows = rows.astype(jnp.float32) >= left_ref[0, n:n + 1]
    left_cols = cols.astype(jnp.float32) < left_ref[1, n:n + 1]
    for k in range(2):
        own = jnp.where(cols >= col0, grad_ref[k, :n], 0.0)
        left = jnp.where(left_cols, left_ref[k, :n], 0.0)
        mine_ref[k] = jnp.where(rows >= row0, own, 0.0) + jnp.where(left_rows, left, 0.0)
        down_ref[k] = jnp.where(rows < row0, own, 0.0) + jnp.where(left_rows, 0.0, left)


def pair_kernel(keep_ref, other_ref, out_ref):
    count, wide, n = keep_ref.shape
    n_x, _, n_y, n_z, eight = out_ref.shape[:5]
    for a in range(count):
        turned = (keep_ref[a] + other_ref[a]).T.reshape(n_z, 2, eight, wide)
        out_ref[a % n_x, 0, a // n_x] = turned[:, 0]
        out_ref[a % n_x, 1, a // n_x] = turned[:, 1]


def patch_kernel(
    inverse_slots, scal_ref, side_ref, beside_ref, probe_ref, amp_ref, ta_ref, tb_ref,
    keep_ref, send_ref, grad_ref,
    patch_s, far_s, grad_s, mid_s,
):
    modes = probe_ref.shape[0]
    n = side_ref.shape[1]
    row0, col0, live, parity = scal_ref[0], scal_ref[1], scal_ref[2], scal_ref[3]
    cols = lax.broadcasted_iota(jnp.int32, (n, n), 1)
    for k in range(2):
        mixed = jnp.where(cols >= col0, side_ref[k], beside_ref[k])
        mixed = pltpu.roll(mixed, (n - row0) % n, 0)
        patch_s[k] = pltpu.roll(mixed, (n - col0) % n, 1)
    xr, xi = patch_s[0], patch_s[1]
    for m in range(modes):
        pr = probe_ref[m, 0].astype(jnp.float32)
        pi = probe_ref[m, 1].astype(jnp.float32)
        er = (pr * xr - pi * xi).astype(jnp.bfloat16)
        ei = (pr * xi + pi * xr).astype(jnp.bfloat16)
        mid = jnp.dot(tb_ref[...], jnp.concatenate([er, ei], 0), preferred_element_type=jnp.float32)
        mid_s[m * n:(m + 1) * n, :n] = mid[:n].astype(jnp.bfloat16)
        mid_s[m * n:(m + 1) * n, n:] = mid[n:].astype(jnp.bfloat16)
    far_s[...] = jnp.dot(mid_s[...], ta_ref[...], preferred_element_type=jnp.float32).reshape(modes, n, 2 * n)
    power = jnp.zeros((n, n), jnp.float32)
    for m in range(modes):
        power = power + (far_s[m, :, :n] * far_s[m, :, :n] + far_s[m, :, n:] * far_s[m, :, n:])
    scale = amp_ref[...] / jnp.maximum(jnp.sqrt(power), 0.5)
    for m in range(modes):
        fr = (far_s[m, :, :n] * scale).astype(jnp.bfloat16)
        fi = (far_s[m, :, n:] * scale).astype(jnp.bfloat16)
        mid = jnp.dot(ta_ref[...], jnp.concatenate([fr, fi], 0), preferred_element_type=jnp.float32)
        mid_s[m * n:(m + 1) * n, :n] = mid[:n].astype(jnp.bfloat16)
        mid_s[m * n:(m + 1) * n, n:] = mid[n:].astype(jnp.bfloat16)
    far_s[...] = jnp.dot(mid_s[...], tb_ref[...], preferred_element_type=jnp.float32).reshape(modes, n, 2 * n)
    live_f = live.astype(jnp.float32)
    part = keep_ref.shape[1] // (2 * modes)
    mean = live_f * inverse_slots
    for a in range(keep_ref.shape[0]):
        for q, out_ref in ((0, keep_ref), (1, send_ref)):
            half = parity if q == 0 else 1 - parity
            here = pl.ds(pl.multiple_of(a * 2 * part + half * part, part), part)
            xr, xi = patch_s[0, here, :], patch_s[1, here, :]
            sr, si = xr * mean, xi * mean
            gr = jnp.zeros_like(xr)
            gi = jnp.zeros_like(xr)
            for m in range(modes):
                pr = probe_ref[m, 0, here, :].astype(jnp.float32)
                pi = probe_ref[m, 1, here, :].astype(jnp.float32)
                dr = (pr * xr - pi * xi) - far_s[m, here, :n]
                di = (pr * xi + pi * xr) - far_s[m, here, n:]
                gr = gr + (pr * dr + pi * di)
                gi = gi + (pr * di - pi * dr)
                out_ref[a, 2 * m * part:(2 * m + 1) * part, :] = sr * dr + si * di
                out_ref[a, (2 * m + 1) * part:(2 * m + 2) * part, :] = sr * di - si * dr
            grad_s[0, here, :] = gr * live_f
            grad_s[1, here, :] = gi * live_f
    for k in range(2):
        grad_ref[k, :n] = pltpu.roll(pltpu.roll(grad_s[k], row0, 0), col0, 1)
        grad_ref[k, n:] = jnp.full((grad_ref.shape[1] - n, n), scal_ref[k], jnp.int32).astype(jnp.float32)


def shards(specimen, probe_modes, amplitude, offsets, counts):
    tile_rows, tile_cols = specimen.shape[1:]
    modes = probe_modes.shape[0]
    n = probe_modes.shape[2]
    n_row, n_col = lax.axis_size(ROW), lax.axis_size(COL)
    slots = n_row * n_col * offsets.shape[2]
    row_id, col_id = lax.axis_index(ROW), lax.axis_index(COL)
    n_x, half = lax.axis_size("x"), n_row // 2
    part = n // n_row

    corner = offsets[0, 0, 0] - jnp.stack([row_id * tile_rows, col_id * tile_cols])
    live = (counts[0, 0] > 0).astype(jnp.int32)
    row0, col0 = corner[0], corner[1]

    vmem = pl.BlockSpec(memory_space=pltpu.VMEM)
    smem = pl.BlockSpec(memory_space=pltpu.SMEM)
    below = shifted(specimen, ROW, -1)
    left_corner = shifted(corner, COL, 1)
    own = pl.pallas_call(
        near_kernel,
        out_shape=jax.ShapeDtypeStruct(specimen.shape, jnp.float32),
        in_specs=[vmem],
        out_specs=vmem,
        compiler_params=pltpu.CompilerParams(vmem_limit_bytes=3 << 20),
    )(specimen)
    mixed = pl.pallas_call(
        mix_kernel,
        out_shape=jax.ShapeDtypeStruct(specimen.shape, jnp.float32),
        in_specs=[smem, vmem, vmem],
        out_specs=vmem,
        compiler_params=pltpu.CompilerParams(vmem_limit_bytes=3 << 20),
    )(left_corner, own, below)
    beside = shifted(mixed, COL, -1)

    scalars = jnp.stack([row0, col0, live, row_id % 2]).astype(jnp.int32)
    table_a, table_b = dft_tables(n)
    operands = (probe_modes, amplitude[0, 0, 0], jnp.asarray(table_a), jnp.asarray(table_b))
    side, *operands = pl.pallas_call(
        side_kernel,
        out_shape=(jax.ShapeDtypeStruct((2, n, n), jnp.float32),)
        + tuple(jax.ShapeDtypeStruct(value.shape, value.dtype) for value in operands),
        in_specs=[smem] + [vmem] * 6,
        out_specs=(vmem,) * 5,
        compiler_params=pltpu.CompilerParams(vmem_limit_bytes=10 << 20),
    )(scalars, own, below, *operands)
    keep, send, grad = pl.pallas_call(
        functools.partial(patch_kernel, 1.0 / slots),
        out_shape=(
            jax.ShapeDtypeStruct((half, 2 * modes * part, n), jnp.float32),
            jax.ShapeDtypeStruct((half, 2 * modes * part, n), jnp.float32),
            jax.ShapeDtypeStruct((2, n + 8, n), jnp.float32),
        ),
        in_specs=[smem] + [vmem] * 6,
        out_specs=(vmem,) * 3,
        scratch_shapes=[
            pltpu.VMEM((2, n, n), jnp.float32),
            pltpu.VMEM((modes, n, 2 * n), jnp.float32),
            pltpu.VMEM((2, n, n), jnp.float32),
            pltpu.VMEM((modes * n, 2 * n), jnp.bfloat16),
        ],
        compiler_params=pltpu.CompilerParams(vmem_limit_bytes=14 << 20),
    )(scalars, side, beside, *operands)

    other = lax.ppermute(send, "core", [(0, 1), (1, 0)])
    from_left = shifted(grad, COL, 1)
    summed = pl.pallas_call(
        pair_kernel,
        out_shape=jax.ShapeDtypeStruct((n_x, 2, half // n_x, n_col // 2, n // n_col, 2 * modes * part), jnp.float32),
        in_specs=[vmem] * 2,
        out_specs=vmem,
        compiler_params=pltpu.CompilerParams(vmem_limit_bytes=8 << 20),
    )(keep, other)
    summed = lax.all_to_all(summed, "x", 0, 0, tiled=True)
    mine, down = pl.pallas_call(
        split_kernel,
        out_shape=(jax.ShapeDtypeStruct((2, n, n), jnp.float32),) * 2,
        in_specs=[smem, vmem, vmem],
        out_specs=(vmem,) * 2,
        compiler_params=pltpu.CompilerParams(vmem_limit_bytes=4 << 20),
    )(scalars, grad, from_left)
    from_above = shifted(down, ROW, 1)
    summed = summed.sum(0).reshape((2 * n_col,) + summed.shape[-2:])
    summed = lax.all_to_all(summed, ("yhi", "ylo", "z"), 0, 0, tiled=True).sum(0)
    probe_grad = summed.T.reshape(modes, 2, part, n // n_col)
    specimen_grad = mine + from_above
    return (specimen_grad, probe_grad)


def solution(mesh):
    n_row, n_col = mesh.devices.shape
    fine = Mesh(mesh.devices.reshape(2, n_row // 4, 2, n_col // 2, 2), ROW + COL)
    in_specs = (
        P(None, ROW, COL),
        P(),
        P(ROW, COL, None, None, None),
        P(ROW, COL, None, None),
        P(ROW, COL),
    )
    out_specs = (P(None, ROW, COL), P(None, None, ROW, COL))
    return jax.shard_map(shards, mesh=fine, in_specs=in_specs, out_specs=out_specs, check_vma=False)
```
